32 devices in a mesh: req: 16 (over z, y, x), head: 2 (over core).
Axes of the slice: x: 2, y: 2, z: 4, core: 2. Of those that a mesh axis runs over, the one named last changes fastest.
Arguments:
- hidden: bfloat16 [128, 4096], P(None, 'req'), may hold values from -6 to 6
- query_key_value_weight: bfloat16 [4096, 8, 768], P('req', 'head'), may hold values from -0.1875 to 0.1875
- output_weight: bfloat16 [4096, 4096], P('head', 'req'), may hold values from -0.375 to 0.375
- kv_pool: bfloat16 [1024, 8, 128, 256], P('req', 'head'), may hold values from -68 to 68
- lengths: int32 [128], P('req'), may hold values from 513 to 2048, as said below
- page_table: int32 [128, 16], P('req'), may hold values from 0 to 79, as said below
- send_slots: int32 [256], P('req'), may hold values from 0 to 63, as said below
Outputs:
- attn_out: bfloat16 [128, 4096], P('head', 'req')
The draws below stay inside these ranges and needn't reach their ends.
Inputs may be any that keep to these rules, and one draw needn't show every extreme that they name: `page_table`: A request's live positions name distinct slots of its group's store, and every other entry is 0. Slots below 64 are the group's own pool rows; slot 64 + s is the page that group s sends to it. Every group uses exactly 8 of the 16 pages sent to it, never for a long request. `send_slots`: every group sends one page to every group; rows whose page the receiver does not use name an arbitrary slot. In 4 of the groups one request is long (more than (15) * 128 tokens); all others hold at most 768 tokens. The new token sits at position lengths[r].
All inputs are finite; a program needn't handle non-finite values.
Results may differ from the reference program's by a relative error of at most 0.018.
Values may be sent and summed in bfloat16 or wider, within the bound.
No kernel may reach another device: no remote copies, remote signals or barrier semaphores. Data moves between devices by JAX's collectives and lax.ppermute only.
A program may use at most 128 MiB of HBM per device.

```python
import jax
import jax.numpy as jnp
from jax import lax

MODEL_WIDTH = 4096
KEY_HEADS = 8
QUERY_PER_KEY = 4
HEAD_SIZE = 128
PAGE_TOKENS = 128
SHORTP = 6
LONG_PAGES = 16
GROUP_REQUESTS = 8
REQUEST_GROUPS = 16
TOTAL_REQUESTS = 128
POOL_PAGES = 64


def plan(key):
    base_key = jax.random.fold_in(key, 4242)
    long_order = jax.random.permutation(jax.random.fold_in(base_key, 1), REQUEST_GROUPS)
    offset_values = jnp.arange(REQUEST_GROUPS, dtype=jnp.int32)
    offset_scores = jax.random.permutation(jax.random.fold_in(base_key, 2), REQUEST_GROUPS).astype(jnp.int32)
    offset_scores = offset_scores - jnp.where((offset_values == 1) | (offset_values == REQUEST_GROUPS // 2), 2 * REQUEST_GROUPS, 0)
    offset_scores = offset_scores - jnp.where(offset_values == REQUEST_GROUPS - 1, REQUEST_GROUPS, 0)
    offsets = jnp.argsort(offset_scores)[:REQUEST_GROUPS // 2].astype(jnp.int32)
    long_rank = jnp.argsort(long_order)

    def home(group_index):
        own_key = jax.random.fold_in(base_key, 1000 + group_index)
        short_len = jax.random.randint(jax.random.fold_in(own_key, 1), (GROUP_REQUESTS,), (SHORTP - 2) * PAGE_TOKENS + 1, SHORTP * PAGE_TOKENS + 1)
        longer = jax.random.randint(jax.random.fold_in(own_key, 2), (), (LONG_PAGES - 1) * PAGE_TOKENS + 1, LONG_PAGES * PAGE_TOKENS + 1)
        longer = jnp.where(long_rank[group_index] == 0, LONG_PAGES * PAGE_TOKENS, longer)
        long_spot = jax.random.randint(jax.random.fold_in(own_key, 3), (), 0, GROUP_REQUESTS)
        is_long = (jnp.arange(GROUP_REQUESTS) == long_spot) & (long_rank[group_index] < REQUEST_GROUPS // 4)
        group_lengths = jnp.where(is_long, longer, short_len)
        places = jnp.arange(LONG_PAGES)
        is_live = places[None, :] * PAGE_TOKENS < group_lengths[:, None]
        movable = (is_live & ~is_long[:, None]).reshape(-1)
        scores = jax.random.permutation(jax.random.fold_in(own_key, 4), GROUP_REQUESTS * LONG_PAGES) + jnp.where(movable, 0, GROUP_REQUESTS * LONG_PAGES)
        picked = jnp.argsort(scores)[:REQUEST_GROUPS // 2]
        sources = (group_index - offsets) % REQUEST_GROUPS
        remote = jnp.zeros((GROUP_REQUESTS * LONG_PAGES,), jnp.bool_).at[picked].set(True)
        remote_src = jnp.zeros((GROUP_REQUESTS * LONG_PAGES,), jnp.int32).at[picked].set(sources.astype(jnp.int32))
        is_local = is_live.reshape(-1) & ~remote
        rank_local = jnp.cumsum(is_local.astype(jnp.int32)) - 1
        pool_order = jax.random.permutation(jax.random.fold_in(own_key, 5), POOL_PAGES)
        local_slot = pool_order[jnp.clip(REQUEST_GROUPS // 2 + rank_local, 0, POOL_PAGES - 1)]
        group_table = jnp.where(remote, POOL_PAGES + remote_src, jnp.where(is_local, local_slot, 0))
        return (group_lengths.astype(jnp.int32), group_table.reshape(GROUP_REQUESTS, LONG_PAGES).astype(jnp.int32))

    def source(group_index):
        own_key = jax.random.fold_in(base_key, 1000 + group_index)
        pool_order = jax.random.permutation(jax.random.fold_in(own_key, 5), POOL_PAGES)
        filler = jax.random.randint(jax.random.fold_in(own_key, 6), (REQUEST_GROUPS,), 0, POOL_PAGES)
        targets = (group_index + offsets) % REQUEST_GROUPS
        return filler.at[targets].set(pool_order[:REQUEST_GROUPS // 2]).astype(jnp.int32)
    all_lengths, all_tables = jax.vmap(home)(jnp.arange(REQUEST_GROUPS))
    all_sends = jax.vmap(source)(jnp.arange(REQUEST_GROUPS))
    return (all_lengths.reshape(-1), all_tables.reshape(-1, LONG_PAGES), all_sends.reshape(-1))


def draw_lengths(key, part):
    return plan(key)[0]


def draw_page_table(key, part):
    return plan(key)[1]


def draw_send_slots(key, part):
    return plan(key)[2]


def draw_kv_pool(key, part):
    shape_of_pool = (REQUEST_GROUPS * POOL_PAGES, KEY_HEADS, PAGE_TOKENS, 2 * HEAD_SIZE)
    values = jnp.clip(jax.random.normal(jax.random.fold_in(key, 1), shape_of_pool, jnp.float32), -4.0, 4.0)
    return values.astype(jnp.bfloat16)


def raised(array, key, source, target, parts, factor):
    owner, partner = [(jnp.arange(array.shape[axis_at]) // (array.shape[axis_at] // parts)).reshape([-1 if axis == axis_at else 1 for axis in range(array.ndim)]) for axis_at in (source, target)]
    chosen = jax.random.permutation(key, parts)[partner]
    strong = (owner == chosen) | (owner == (partner + parts // 2) % parts)
    return jnp.where(strong, factor * array, array)


def levels(stream_key, extent, split, least, top_value):
    def one(position, parts):
        draws = jax.random.uniform(jax.random.fold_in(jax.random.fold_in(stream_key, 6), position), (parts,), jnp.float32, least / len(split), top_value / len(split))
        return jnp.repeat(jnp.exp(draws), extent[position] // parts).reshape((-1,) + (1,) * (len(extent) - position - 1))

    loudness = one(*split[0])
    for cut in split[1:]:
        loudness = loudness * one(*cut)
    return loudness


def bell_draw(rng, shape, scale, reach, cuts=(), kind=jnp.bfloat16):
    values = scale * jax.random.normal(rng, shape, jnp.float32)
    if cuts:
        values = values * levels(rng, shape, cuts, -0.22, 0.18)
    return jnp.clip(values, -reach, reach).astype(kind)


def gaussian_with(stream_key, extent, spread, limit, cuts, heavy, kind=jnp.bfloat16):
    array = spread * jax.random.normal(stream_key, extent, jnp.float32)
    if cuts:
        array = array * levels(stream_key, extent, cuts, -0.22, 0.18)
    return jnp.clip(raised(array, jax.random.fold_in(stream_key, 3), *heavy), -limit, limit).astype(kind)


def setup_inputs(seed: int = 0) -> dict:
    key_of = jax.random.split(jax.random.key(seed), 8)
    hidden = gaussian_with(key_of[0], (TOTAL_REQUESTS, MODEL_WIDTH), 1.0, 6.0, ((1, 16),), (1, 0, 16, 2.0))
    query_key_value_weight = bell_draw(key_of[1], (MODEL_WIDTH, KEY_HEADS, (QUERY_PER_KEY + 2) * HEAD_SIZE), (MODEL_WIDTH // 4) ** -0.5, 0.1875, ((0, 16), (1, 2)))
    output_weight = bell_draw(key_of[2], (KEY_HEADS * QUERY_PER_KEY * HEAD_SIZE, MODEL_WIDTH), 256 ** -0.5, 0.375, ((0, 2), (1, 16)))
    kv_pool = draw_kv_pool(jax.random.fold_in(key_of[7], 71), 0)
    lengths = draw_lengths(jax.random.fold_in(key_of[7], 71), 0)
    page_table = draw_page_table(jax.random.fold_in(key_of[7], 71), 0)
    send_slots = draw_send_slots(jax.random.fold_in(key_of[7], 71), 0)
    return {"hidden": hidden, "query_key_value_weight": query_key_value_weight, "output_weight": output_weight, "kv_pool": kv_pool, "lengths": lengths, "page_table": page_table, "send_slots": send_slots}


ROPE_BASE = 500000.0
NEG_FILL = -1e30


def rotate(vectors, angles):
    half_width = vectors.shape[-1] // 2
    first_half = vectors[..., :half_width]
    second_half = vectors[..., half_width:]
    cosine = jnp.cos(angles)
    sine_part = jnp.sin(angles)
    return jnp.concatenate([first_half * cosine - second_half * sine_part, second_half * cosine + first_half * sine_part], axis=-1)


def rope_angles(lengths, width):
    exponent = jnp.arange(width // 2, dtype=jnp.float32) * (2.0 / width)
    inverse = 1.0 / (ROPE_BASE ** exponent)
    return lengths.astype(jnp.float32)[:, None] * inverse[None, :]


def split_projection(projected_rows, lengths):
    angles = rope_angles(lengths, projected_rows.shape[-1])
    queries = rotate(projected_rows[:, :, :-2], angles[:, None, None, :]).astype(jnp.bfloat16)
    new_keys = rotate(projected_rows[:, :, -2], angles[:, None, :]).astype(jnp.bfloat16)
    new_values = projected_rows[:, :, -1].astype(jnp.bfloat16)
    return queries, new_keys, new_values


def page_stats(queries, keys, values, valid_tokens):
    score_scale = queries.shape[-1] ** -0.5
    scores = jnp.einsum("abhqd,abhtd->abhqt", queries.astype(jnp.float32), keys.astype(jnp.float32)) * score_scale
    token_mask = jnp.arange(keys.shape[-2]) < valid_tokens[:, :, None, None, None]
    masked = jnp.where(token_mask, scores, NEG_FILL)
    top_score = jnp.max(masked, axis=-1)
    weights = jnp.where(token_mask, jnp.exp(scores - top_score[..., None]), 0.0)
    weight_sum = jnp.sum(weights, axis=-1)
    rounded = lax.optimization_barrier(weights.astype(jnp.bfloat16))
    weighted_values = jnp.einsum("abhqt,abhtd->abhqd", rounded.astype(jnp.float32), values.astype(jnp.float32))
    return top_score, weight_sum, weighted_values


def reference(hidden, query_key_value_weight, output_weight, kv_pool, lengths, page_table, send_slots):
    projected_rows = jnp.dot(hidden, query_key_value_weight.reshape(MODEL_WIDTH, KEY_HEADS * (QUERY_PER_KEY + 2) * HEAD_SIZE), preferred_element_type=jnp.float32)
    projected_rows = projected_rows.reshape(TOTAL_REQUESTS, KEY_HEADS, QUERY_PER_KEY + 2, HEAD_SIZE)
    queries, new_keys, new_values = split_projection(projected_rows, lengths)
    score_scale = HEAD_SIZE ** -0.5
    self_scores = jnp.sum(queries.astype(jnp.float32) * new_keys.astype(jnp.float32)[:, :, None, :], axis=-1) * score_scale

    def single_group(group_index):
        first_row = (group_index * GROUP_REQUESTS).astype(jnp.int32)
        group_table = lax.dynamic_slice_in_dim(page_table, first_row, GROUP_REQUESTS, 0)
        group_lengths = lax.dynamic_slice_in_dim(lengths, first_row, GROUP_REQUESTS, 0)
        grouped_query_rows = lax.dynamic_slice_in_dim(queries, first_row, GROUP_REQUESTS, 0)
        group_self = lax.dynamic_slice_in_dim(self_scores, first_row, GROUP_REQUESTS, 0)
        group_values = lax.dynamic_slice_in_dim(new_values, first_row, GROUP_REQUESTS, 0)
        is_remote = group_table >= POOL_PAGES
        source = jnp.clip(group_table - POOL_PAGES, 0, REQUEST_GROUPS - 1).astype(jnp.int32)
        remote_slot = send_slots[source * REQUEST_GROUPS + group_index]
        global_index = jnp.where(is_remote, source * POOL_PAGES + remote_slot, group_index * POOL_PAGES + group_table).astype(jnp.int32)
        group_pages = kv_pool[global_index]
        places = jnp.arange(LONG_PAGES, dtype=jnp.int32)
        valid_tokens = jnp.clip(group_lengths[:, None] - places[None, :] * PAGE_TOKENS, 0, PAGE_TOKENS)
        scattered_queries = jnp.broadcast_to(grouped_query_rows[:, None], (GROUP_REQUESTS, LONG_PAGES, KEY_HEADS, QUERY_PER_KEY, HEAD_SIZE))
        page_max, page_sum, page_acc = page_stats(scattered_queries, group_pages[..., :HEAD_SIZE], group_pages[..., HEAD_SIZE:], valid_tokens)
        top_score = jnp.maximum(jnp.max(page_max, axis=1), group_self)
        factors = jnp.exp(page_max - top_score[:, None])
        self_weight = jnp.exp(group_self - top_score)
        total_weight_sum = jnp.sum(factors * page_sum, axis=1) + self_weight
        weighted_values = jnp.sum(factors[..., None] * page_acc, axis=1) + self_weight[..., None] * group_values.astype(jnp.float32)[:, :, None, :]
        return (weighted_values / total_weight_sum[..., None]).astype(jnp.bfloat16).reshape(GROUP_REQUESTS, KEY_HEADS * QUERY_PER_KEY * HEAD_SIZE)

    output_per_head = lax.map(single_group, jnp.arange(REQUEST_GROUPS, dtype=jnp.int32)).reshape(TOTAL_REQUESTS, KEY_HEADS * QUERY_PER_KEY * HEAD_SIZE)
    return jnp.dot(output_per_head, output_weight, preferred_element_type=jnp.float32).astype(jnp.bfloat16)
```

```python
import functools

import jax
import jax.numpy as jnp
from jax import lax
from jax.experimental import pallas as pl
from jax.experimental.pallas import tpu as pltpu
from jax.sharding import PartitionSpec as P

ROPE_BASE = 500000.0
NEG_FILL = -1e30
SHORT_TOKENS = 768
ROW_TILE = 16
LANES = 128


def vmem():
    return pl.BlockSpec(memory_space=pltpu.VMEM)


def smem():
    return pl.BlockSpec(memory_space=pltpu.SMEM)


def params(mib):
    return pltpu.CompilerParams(vmem_limit_bytes=mib * 2**20)


def rope_tables(lengths, width):
    exponent = jnp.arange(width // 2, dtype=jnp.float32) * (2.0 / width)
    inverse = 1.0 / ROPE_BASE**exponent
    angles = lengths.astype(jnp.float32)[:, None] * inverse[None, :]
    cosine = jnp.cos(angles)
    sine = jnp.sin(angles)
    return (
        jnp.concatenate([cosine, cosine], axis=1),
        jnp.concatenate([-sine, sine], axis=1),
    )


def prep_kernel(
    heads, per_head, rows, groups,
    owner, valid, sharing, arrived, cosine, sine,
    queries, self_scores, new_values, payload,
):
    width = cosine.shape[1]
    scale = width**-0.5
    per_key = per_head - 2
    count = cosine.shape[0]
    cos = cosine[...]
    sin = sine[...]

    def projected(column):
        lanes = pl.ds(column * width, width)
        total = arrived[0:ROW_TILE, lanes].astype(jnp.float32)
        for start in range(ROW_TILE, groups * count, ROW_TILE):
            total = total + arrived[start : start + ROW_TILE, lanes].astype(jnp.float32)
        summed = total[:count]
        for start in range(count, ROW_TILE, count):
            summed = summed + total[start : start + count]
        return summed

    def rounded(value):
        return value.astype(jnp.bfloat16).astype(jnp.float32)

    def rotated(column):
        value = projected(column)
        return rounded(value * cos + pltpu.roll(value, width // 2, 1) * sin)

    if rows > heads * per_key:
        queries[...] = jnp.zeros(queries.shape, jnp.float32)
        self_scores[...] = jnp.zeros(queries.shape, jnp.float32)
        new_values[...] = jnp.zeros(queries.shape, jnp.float32)
    for head in range(heads):
        base = head * per_head
        key = rotated(base + per_key)
        value = rounded(projected(base + per_key + 1))
        for j in range(per_key):
            query = rotated(base + j)
            score = jnp.sum(query * key, axis=1, keepdims=True) * scale
            row = head * per_key + j
            queries[:, row, :] = query
            self_scores[:, row, :] = jnp.broadcast_to(score, query.shape)
            new_values[:, row, :] = value
    fill_payload(groups, rows, owner, valid, sharing, queries, payload)


def fill_payload(groups, rows, owner, valid, sharing, queries, payload):
    width = queries.shape[2]
    lane = lax.broadcasted_iota(jnp.int32, (rows, LANES), 1)

    def fill(s, carry):
        query = queries[jnp.maximum(owner[s], 0)]
        tokens = valid[s].astype(jnp.float32)
        shared = sharing[0].astype(jnp.float32)
        extra = jnp.where(lane == 0, tokens, jnp.where(lane == 1, shared, 0.0))
        at = pl.ds(pl.multiple_of(s * rows, ROW_TILE), rows)
        payload[at, 0:width] = query.astype(jnp.bfloat16)
        payload[at, width : width + LANES] = extra.astype(jnp.bfloat16)
        return carry

    lax.fori_loop(0, groups, fill, 0, unroll=groups <= 16)


def payload_kernel(groups, rows, owner, valid, sharing, queries, payload):
    fill_payload(groups, rows, owner, valid, sharing, queries, payload)


def head_pairs(heads):
    return [list(range(h, min(h + 2, heads))) for h in range(0, heads, 2)]


def spread(query, heads, per_key):
    row = lax.broadcasted_iota(jnp.int32, query.shape, 0)
    pieces = [
        jnp.where((row >= h * per_key) & (row < (h + 1) * per_key), query, 0.0)
        for h in range(heads)
    ]
    return jnp.concatenate(pieces, axis=1).astype(jnp.bfloat16)


def pick(product, first, members, per_key, width):
    row = lax.broadcasted_iota(jnp.int32, (product.shape[0], width), 0)
    total = None
    for i, h in enumerate(members):
        piece = product[:, i * width : (i + 1) * width]
        piece = jnp.where((row >= h * per_key) & (row < (h + 1) * per_key), piece, 0.0)
        total = piece if total is None else total + piece
    return total


def attend(query, pages, slots, masks, state, heads, per_key):
    width = query.shape[1]
    scale = width**-0.5
    spread_query = spread(query, heads, per_key)
    couples = [slots[i : i + 2] for i in range(0, len(slots), 2)]

    def block(couple, members, lanes):
        return jnp.concatenate(
            [jnp.concatenate([pages[s, h, :, lanes] for h in members], axis=1) for s in couple],
            axis=0,
        )

    scores = []
    for couple in couples:
        total = None
        for members in head_pairs(heads):
            part = lax.dot_general(
                spread_query[:, members[0] * width : (members[-1] + 1) * width],
                block(couple, members, slice(0, width)),
                (((1,), (1,)), ((), ())),
                preferred_element_type=jnp.float32,
            )
            total = part if total is None else total + part
        scores.append(total)
    mask = jnp.concatenate(masks, axis=1)
    scores = jnp.where(mask, jnp.concatenate(scores, axis=1) * scale, NEG_FILL)
    old_max, old_sum, old_acc = state
    top = jnp.maximum(old_max, jnp.max(scores, axis=1, keepdims=True))
    weights = jnp.where(mask, jnp.exp(scores - top), 0.0)
    fade = jnp.exp(old_max - top)
    total_sum = fade * old_sum + jnp.sum(weights, axis=1, keepdims=True)
    weights = weights.astype(jnp.bfloat16)
    acc = fade * old_acc
    for members in head_pairs(heads):
        product = None
        at = 0
        for couple in couples:
            values = block(couple, members, slice(width, 2 * width))
            part = jnp.dot(
                weights[:, at : at + values.shape[0]], values, preferred_element_type=jnp.float32
            )
            at += values.shape[0]
            product = part if product is None else product + part
        acc = acc + pick(product, members[0], members, per_key, width)
    return top, total_sum, acc


def local_kernel(
    first, main, heads, per_key,
    table, lengths, queries, self_scores, new_values, pool,
    maxima, sums, accs, pages, sems,
):
    count = maxima.shape[0]
    positions = table.shape[1]
    pool_slots = pool.shape[0]
    page_len = pool.shape[2]
    rows = queries.shape[1]
    extra = positions - main
    overflow = count * main

    def copy(request, position, slot):
        entry = table[first + request, position]
        source = jnp.where(entry < pool_slots, entry, 0)
        return pltpu.make_async_copy(pool.at[source], pages.at[slot], sems.at[slot])

    def is_long(request):
        return lengths[first + request] > main * page_len

    def start_main(i, carry):
        copy(i // main, i % main, i).start()
        return carry

    lax.fori_loop(0, count * main, start_main, 0)

    def start_extra(request, carry):
        @pl.when(is_long(request))
        def _():
            for i in range(extra):
                copy(request, main + i, overflow + i).start()

        return carry

    if extra > 0:
        lax.fori_loop(0, count, start_extra, 0)

    token = lax.broadcasted_iota(jnp.int32, (rows, page_len), 1)

    def mask_of(request, position):
        entry = table[first + request, position]
        left = lengths[first + request] - position * page_len
        return token < jnp.where(entry < pool_slots, left, 0)

    def update(request, begin, end, slot, state):
        slots = [slot + i for i in range(end - begin)]
        for i, s in enumerate(slots):
            copy(request, begin + i, s).wait()
        masks = [mask_of(request, p) for p in range(begin, end)]
        query = queries[first + request]
        return attend(query, pages, slots, masks, state, heads, per_key)

    def store(request, state):
        maxima[request] = jnp.broadcast_to(state[0], maxima.shape[1:])
        sums[request] = jnp.broadcast_to(state[1], sums.shape[1:])
        accs[request] = state[2]

    def one(request, carry):
        begin = (
            self_scores[first + request][:, 0:1],
            jnp.ones((rows, 1), jnp.float32),
            new_values[first + request],
        )
        store(request, update(request, 0, main, request * main, begin))
        if extra > 0:

            @pl.when(is_long(request))
            def _():
                state = (maxima[request][:, 0:1], sums[request][:, 0:1], accs[request])
                store(request, update(request, main, positions, overflow, state))

        return carry

    lax.fori_loop(0, count, one, 0)


def remote_kernel(heads, per_key, rows, slots, payload, pool, result, pages, sems):
    groups = slots.shape[0]
    page_len = pool.shape[2]
    width = pool.shape[3] // 2
    depth = pages.shape[0]

    def copy(s):
        return pltpu.make_async_copy(
            pool.at[slots[s]], pages.at[lax.rem(s, depth)], sems.at[lax.rem(s, depth)]
        )

    def start(s, carry):
        copy(s).start()
        return carry

    lax.fori_loop(0, depth, start, 0)
    token = lax.broadcasted_iota(jnp.int32, (rows, page_len), 1).astype(jnp.float32)
    lane = lax.broadcasted_iota(jnp.int32, (rows, LANES), 1)

    def one(s, carry):
        copy(s).wait()
        at = pl.ds(pl.multiple_of(s * rows, ROW_TILE), rows)
        packed = payload[at, :].astype(jnp.float32)
        query = packed[:, 0:width]
        tokens = packed[:, width : width + 1]
        empty = (
            jnp.full((rows, 1), NEG_FILL, jnp.float32),
            jnp.zeros((rows, 1), jnp.float32),
            jnp.zeros((rows, width), jnp.float32),
        )
        top, total, acc = attend(
            query, pages, [lax.rem(s, depth)], [token < tokens], empty, heads, per_key
        )
        used = total > 0.0
        level = jnp.where(used, top + jnp.log(jnp.where(used, total, 1.0)), NEG_FILL)
        high = level.astype(jnp.bfloat16).astype(jnp.float32)
        middle = (level - high).astype(jnp.bfloat16).astype(jnp.float32)
        low = level - high - middle
        stats = jnp.where(
            lane == 0, high, jnp.where(lane == 1, middle, jnp.where(lane == 2, low, 0.0))
        )
        mean = acc / jnp.where(used, total, 1.0)
        result[at, 0:width] = mean.astype(jnp.bfloat16)
        result[at, width : width + LANES] = stats.astype(jnp.bfloat16)

        @pl.when(s + depth < groups)
        def _():
            copy(s + depth).start()

        return carry

    lax.fori_loop(0, groups, one, 0)


def combine_kernel(
    parts, rows, real_rows, final, owner, arrived, *refs
):
    inputs = refs[: 3 * parts]
    outputs = refs[3 * parts : -3]
    maxima, sums, accs = refs[-3:]
    groups = owner.shape[0]
    width = accs.shape[2]
    per_part = accs.shape[0] // parts
    for i in range(parts):
        at = slice(i * per_part, (i + 1) * per_part)
        maxima[at] = inputs[3 * i][...]
        sums[at] = inputs[3 * i + 1][...]
        accs[at] = inputs[3 * i + 2][...]

    def merge(s, carry):
        request = owner[s]

        @pl.when(request >= 0)
        def _():
            at = pl.ds(pl.multiple_of(s * rows, ROW_TILE), rows)
            packed = arrived[at, :].astype(jnp.float32)
            level = (
                packed[:, width : width + 1]
                + packed[:, width + 1 : width + 2]
                + packed[:, width + 2 : width + 3]
            )
            old = maxima[request]
            top = jnp.maximum(old, level)
            fade = jnp.exp(old - top)
            gain = jnp.exp(level - top)
            maxima[request] = top
            sums[request] = fade * sums[request] + gain
            accs[request] = fade * accs[request] + gain * packed[:, 0:width]

        return carry

    lax.fori_loop(0, groups, merge, 0)
    if final:
        for row in range(real_rows):
            outputs[0][:, row * width : (row + 1) * width] = (
                accs[:, row, :] / sums[:, row, :]
            ).astype(jnp.bfloat16)
    else:
        for ref, held in zip(outputs, (maxima, sums, accs)):
            ref[...] = held[...]


def shards(hidden, query_key_value_weight, output_weight, kv_pool, lengths, page_table, send_slots):
    groups = lax.axis_size("req")
    count = lengths.shape[0]
    heads = query_key_value_weight.shape[1]
    pool_slots, _, page_len, pair_width = kv_pool.shape
    width = pair_width // 2
    per_head = query_key_value_weight.shape[2] // width
    per_key = per_head - 2
    real_rows = heads * per_key
    rows = -(-real_rows // ROW_TILE) * ROW_TILE
    positions = page_table.shape[1]
    main = min(SHORT_TOKENS // page_len, positions)
    page_bytes = heads * page_len * pair_width * 2
    f32 = jnp.float32
    bf16 = jnp.bfloat16

    flat_weight = query_key_value_weight.reshape(
        query_key_value_weight.shape[0], heads * per_head * width
    )
    partial = jnp.dot(hidden, flat_weight, preferred_element_type=f32).astype(bf16)
    arrived = lax.all_to_all(partial, "req", split_axis=0, concat_axis=0, tiled=True)

    places = jnp.arange(positions, dtype=jnp.int32)
    tokens_in = jnp.clip(lengths[:, None] - places[None, :] * page_len, 0, page_len)
    sources = jnp.arange(groups, dtype=jnp.int32)
    hits = (page_table[:, :, None] == pool_slots + sources[None, None, :]) & (
        tokens_in[:, :, None] > 0
    )
    uses = jnp.any(hits, axis=1)
    tokens_used = jnp.sum(jnp.where(hits, tokens_in[:, :, None], 0), axis=1)
    before = jnp.cumsum(uses.astype(jnp.int32), axis=0)
    requests = jnp.arange(count, dtype=jnp.int32)

    def turn(index):
        chosen = uses & (before == index + 1)
        owner = jnp.where(
            jnp.any(chosen, axis=0), jnp.sum(jnp.where(chosen, requests[:, None], 0), axis=0), -1
        )
        return owner, jnp.sum(jnp.where(chosen, tokens_used, 0), axis=0)

    owner, valid = turn(0)
    sharing = jnp.max(before[-1]).reshape(1)
    cosine, sine = rope_tables(lengths, width)

    state_shape = jax.ShapeDtypeStruct((count, rows, width), f32)
    payload_shape = jax.ShapeDtypeStruct((groups * rows, width + LANES), bf16)
    queries, self_scores, new_values, payload = pl.pallas_call(
        functools.partial(prep_kernel, heads, per_head, rows, groups),
        out_shape=(state_shape, state_shape, state_shape, payload_shape),
        in_specs=[smem(), smem(), smem(), vmem(), vmem(), vmem()],
        out_specs=(vmem(), vmem(), vmem(), vmem()),
        compiler_params=params(16),
        cost_estimate=pl.CostEstimate(
            flops=2 * partial.size, bytes_accessed=4 * partial.size, transcendentals=0
        ),
        name="prep",
    )(owner, valid, sharing, arrived, cosine, sine)

    def exchange(rows_out):
        return lax.all_to_all(rows_out, "req", split_axis=0, concat_axis=0, tiled=True)

    def local(first, size):
        shape = jax.ShapeDtypeStruct((size, rows, width), f32)
        slots = size * main + positions - main
        return pl.pallas_call(
            functools.partial(local_kernel, first, main, heads, per_key),
            out_shape=(shape, shape, shape),
            in_specs=[smem(), smem(), vmem(), vmem(), vmem(), pl.BlockSpec(memory_space=pl.ANY)],
            out_specs=(vmem(), vmem(), vmem()),
            scratch_shapes=[
                pltpu.VMEM((slots,) + kv_pool.shape[1:], bf16),
                pltpu.SemaphoreType.DMA((slots,)),
            ],
            compiler_params=params(24),
            cost_estimate=pl.CostEstimate(
                flops=4 * rows * slots * page_len * width * heads,
                bytes_accessed=2 * slots * page_bytes,
                transcendentals=rows * slots * page_len,
            ),
            name="local_pages",
        )(page_table, lengths, queries, self_scores, new_values, kv_pool)

    depth = min(groups, 16)

    def remote(asked):
        return pl.pallas_call(
            functools.partial(remote_kernel, heads, per_key, rows),
            out_shape=payload_shape,
            in_specs=[smem(), vmem(), pl.BlockSpec(memory_space=pl.ANY)],
            out_specs=vmem(),
            scratch_shapes=[
                pltpu.VMEM((depth,) + kv_pool.shape[1:], bf16),
                pltpu.SemaphoreType.DMA((depth,)),
            ],
            compiler_params=params(16),
            cost_estimate=pl.CostEstimate(
                flops=4 * rows * groups * page_len * width * heads,
                bytes_accessed=2 * groups * page_bytes,
                transcendentals=rows * groups * page_len,
            ),
            name="asked_pages",
        )(send_slots, asked, kv_pool)

    def combine(owner, answers, states, final):
        outs = (
            jax.ShapeDtypeStruct((count, real_rows * width), bf16)
            if final
            else (state_shape, state_shape, state_shape)
        )
        flat = [array for state in states for array in state]
        return pl.pallas_call(
            functools.partial(combine_kernel, len(states), rows, real_rows, final),
            out_shape=outs,
            in_specs=[smem(), vmem()] + [vmem()] * len(flat),
            out_specs=vmem() if final else (vmem(), vmem(), vmem()),
            scratch_shapes=[pltpu.VMEM(state_shape.shape, f32)] * 3,
            compiler_params=params(16),
            name="combine",
        )(owner, answers, *flat)

    asked = exchange(payload)
    half = count // 2
    early = local(0, half)
    answers = exchange(remote(asked))
    late = local(half, count - half)

    rounds = jnp.max(asked.reshape(groups, rows, width + LANES)[:, 0, width + 1]).astype(jnp.int32)

    def one_round(states):
        return combine(owner, answers, states, True)

    def more_rounds(states):
        def body(index, state):
            owner, valid = turn(index)
            payload = pl.pallas_call(
                functools.partial(payload_kernel, groups, rows),
                out_shape=payload_shape,
                in_specs=[smem(), smem(), smem(), vmem()],
                out_specs=vmem(),
                compiler_params=params(16),
                name="payload",
            )(owner, valid, sharing, queries)
            return combine(owner, exchange(remote(exchange(payload))), [state], False)

        state = combine(owner, answers, states, False)
        state = lax.fori_loop(1, rounds, body, state)
        nobody = jnp.full_like(owner, -1)
        return combine(nobody, answers, [state], True)

    output_per_head = lax.cond(rounds > 1, more_rounds, one_round, [early, late])
    partial_out = jnp.dot(
        lax.all_gather(output_per_head, "req", axis=0, tiled=True),
        output_weight,
        preferred_element_type=f32,
    )
    return lax.psum_scatter(partial_out.astype(bf16), "head", scatter_dimension=0, tiled=True)


def solution(mesh):
    return jax.shard_map(
        shards,
        mesh=mesh,
        in_specs=(
            P(None, "req"),
            P("req", "head", None),
            P("head", "req"),
            P("req", "head", None, None),
            P("req"),
            P("req", None),
            P("req"),
        ),
        out_specs=P("head", "req"),
        check_vma=False,
    )
```
